32 devices in a mesh: group: 2 (over y), seq: 16 (over z, x, core).
Axes of the slice: x: 2, y: 2, z: 4, core: 2. Of those that a mesh axis runs over, the one named last changes fastest.
Arguments:
- coarse_query: bfloat16 [1024, 3072], P(('group', 'seq')), parts along dimension 0, may hold values from -96 to 96
- coarse_key: bfloat16 [1024, 3072], P(('group', 'seq')), parts along dimension 0, may hold values from -12 to 12
- coarse_value: bfloat16 [1024, 3072], P(('group', 'seq')), parts along dimension 0, may hold values from -6 to 6
- fine_query: bfloat16 [4096, 3072], P(('group', 'seq')), parts along dimension 0, may hold values from -108 to 108
- fine_key: bfloat16 [4096, 3072], P(('group', 'seq')), parts along dimension 0, may hold values from -9 to 9
- fine_value: bfloat16 [4096, 3072], P(('group', 'seq')), parts along dimension 0, may hold values from -6 to 6
- head_reach: int32 [24], replicated, may hold values from 1 to 2, as said below
Outputs:
- fine_result: bfloat16 [4096, 3072], P(('group', 'seq')), parts along dimension 0
- cross_result: bfloat16 [4096, 3072], P(('group', 'seq')), parts along dimension 0
The draws below stay inside these ranges and needn't reach their ends.
There are 2 independent parts, one for each index of `group`. The reference program is written for one: setup_inputs(seed, part) draws one part's arguments, and reference() takes and returns one part's arrays. A program takes and returns all parts, laid end to end along the dimension named above; an argument that names none is the same for every part. Nothing has to cross between parts.
Inputs may be any that keep to these rules, and one draw needn't show every extreme that they name: `head_reach`: each head reaches at least one frame; some head reaches 2 frames.
All inputs are finite; a program needn't handle non-finite values.
Results may differ from the reference program's by a relative error of at most 0.0054.
Values may be sent and summed in bfloat16 or wider, within the bound.
A program may use at most 128 MiB of HBM per device.

```python
import math
import jax
import jax.numpy as jnp
from jax import lax

D = 3072
HEADS = 24
HD = 128
TT = 4
TH = 4
TW = 8
NT = 8
HALO_F = 2
NS = 2
F_DEV = 128
C_DEV = 32
LC = 512
LF = 2048
FRAMES = 32
N_SEQ = 16


def paired_rows(key, row_count, column_count, deviation, variant):
    bound = 6.0 * deviation
    key_noise = jax.random.normal(jax.random.fold_in(key, variant + 1), (row_count, column_count), jnp.float32)
    key_rows = jnp.clip(deviation * key_noise, -bound, bound)
    query_noise = jax.random.normal(jax.random.fold_in(key, variant + 2), (row_count, column_count), jnp.float32)
    queries = jnp.clip(deviation * query_noise, -bound, bound)
    return (queries, key_rows)


def draw_coarse_query(key, part):
    return paired_rows(key, LC, D, 2.0, 100)[0].astype(jnp.bfloat16)


def draw_coarse_key(key, part):
    return paired_rows(key, LC, D, 2.0, 100)[1].astype(jnp.bfloat16)


def draw_fine_query(key, part):
    return paired_rows(key, LF, D, 1.5, 200)[0].astype(jnp.bfloat16)


def draw_fine_key(key, part):
    return paired_rows(key, LF, D, 1.5, 200)[1].astype(jnp.bfloat16)


def draw_head_reach(key, part):
    reaches = jax.random.randint(jax.random.fold_in(key, 301), (HEADS,), 1, HALO_F + 1)
    ordering = jax.random.permutation(jax.random.fold_in(key, 302), HEADS)
    reaches = reaches.at[ordering[0]].set(HALO_F)
    reaches = reaches.at[ordering[1]].set(1)
    return reaches.astype(jnp.int32)


def block_scale(rng, extent, split, least, top_value):
    def one(position, shards_of):
        heights = jax.random.uniform(jax.random.fold_in(jax.random.fold_in(rng, 6), position), (shards_of,), jnp.float32, least / len(split), top_value / len(split))
        return jnp.repeat(jnp.exp(heights), extent[position] // shards_of).reshape((-1,) + (1,) * (len(extent) - position - 1))

    loudness = one(*split[0])
    for cut in split[1:]:
        loudness = loudness * one(*cut)
    return loudness


def bell_draw(own_key, shape, scale, most, pieces=(), kind=jnp.bfloat16):
    drawn = scale * jax.random.normal(own_key, shape, jnp.float32)
    if pieces:
        drawn = drawn * block_scale(own_key, shape, pieces, -0.22, 0.18)
    return jnp.clip(drawn, -most, most).astype(kind)


def setup_inputs(seed: int = 0, part: int = 0) -> dict:
    keys = jax.random.split(jax.random.key(seed), 8)
    part_keys = jax.random.split(jax.random.fold_in(keys[7], part), 8)
    coarse_query = draw_coarse_query(jax.random.fold_in(jax.random.fold_in(keys[7], part), 71), part)
    coarse_key = draw_coarse_key(jax.random.fold_in(jax.random.fold_in(keys[7], part), 71), part)
    coarse_value = bell_draw(part_keys[2], (LC, D), 1.0, 6.0, ((0, 16),))
    fine_query = draw_fine_query(jax.random.fold_in(jax.random.fold_in(keys[7], part), 71), part)
    fine_key = draw_fine_key(jax.random.fold_in(jax.random.fold_in(keys[7], part), 71), part)
    fine_value = bell_draw(part_keys[5], (LF, D), 1.0, 6.0, ((0, 16),))
    head_reach = draw_head_reach(jax.random.fold_in(keys[7], 71), part)
    return {"coarse_query": coarse_query, "coarse_key": coarse_key, "coarse_value": coarse_value, "fine_query": fine_query, "fine_key": fine_key, "fine_value": fine_value, "head_reach": head_reach}


masked_score = -1e30


def softmax_rows(scores):
    largest = jnp.max(scores, axis=-1, keepdims=True)
    exponent = jnp.exp(scores - largest)
    return (exponent / jnp.sum(exponent, axis=-1, keepdims=True)).astype(jnp.bfloat16)


def attend_heads(query_rows, key_rows, value_rows, allowed):
    head_total = query_rows.shape[1] // HD
    query_heads = query_rows.reshape(query_rows.shape[0], head_total, HD).astype(jnp.float32)
    key_heads = key_rows.reshape(key_rows.shape[0], head_total, HD).astype(jnp.float32)
    value_heads = value_rows.reshape(value_rows.shape[0], head_total, HD).astype(jnp.float32)
    scores = jnp.einsum("qhd,khd->hqk", query_heads, key_heads, precision=lax.Precision.HIGHEST) * (HD ** -0.5)
    if allowed is not None:
        scores = jnp.where(allowed, scores, masked_score)
    weights = softmax_rows(scores).astype(jnp.float32)
    blended = jnp.einsum("hqk,khd->qhd", weights, value_heads, precision=lax.Precision.HIGHEST)
    return blended.reshape(query_rows.shape[0], head_total * HD)


def pool_frames(coarse_rows):
    cells = (TH // 2) * (TW // 2)
    summed = jnp.sum(coarse_rows.reshape(-1, cells, D).astype(jnp.float32), axis=1)
    return summed * (cells ** -0.5)


def reference(coarse_query, coarse_key, coarse_value, fine_query, fine_key, fine_value, head_reach):
    block_rows = math.gcd(LC, 1024)

    def one_head(head_index):
        first_column = head_index * HD
        query_columns = lax.dynamic_slice_in_dim(coarse_query, first_column, HD, 1)
        key_columns = lax.dynamic_slice_in_dim(coarse_key, first_column, HD, 1)
        value_columns = lax.dynamic_slice_in_dim(coarse_value, first_column, HD, 1)

        def one_block(query_block):
            scores = jnp.dot(query_block, key_columns.T, preferred_element_type=jnp.float32) * (HD ** -0.5)
            weights = softmax_rows(scores)
            return jnp.dot(weights, value_columns, preferred_element_type=jnp.float32).astype(jnp.bfloat16)

        return lax.map(one_block, query_columns.reshape(LC // block_rows, block_rows, HD)).reshape(LC, HD)

    per_head = lax.map(one_head, jnp.arange(HEADS, dtype=jnp.int32))
    coarse_attention = per_head.transpose(1, 0, 2).reshape(LC, D)
    pooled_key = pool_frames(coarse_key)
    pooled_value = pool_frames(coarse_value)
    plane_cells = TH * TW
    key_tiles = jnp.pad(fine_key.reshape(NT, NS, F_DEV, D), ((1, 1), (0, 0), (0, 0), (0, 0)))
    value_tiles = jnp.pad(fine_value.reshape(NT, NS, F_DEV, D), ((1, 1), (0, 0), (0, 0), (0, 0)))
    query_tiles = fine_query.reshape(N_SEQ, F_DEV, D)
    coarse_tiles = coarse_attention.reshape(N_SEQ, C_DEV, D)
    zero_index = jnp.int32(0)

    def one_tile(tile_index):
        time_block = (tile_index // NS).astype(jnp.int32)
        region = (tile_index % NS).astype(jnp.int32)
        query_rows = lax.dynamic_index_in_dim(query_tiles, tile_index, 0, keepdims=False)
        window_key = lax.dynamic_slice(key_tiles, (time_block, region, zero_index, zero_index), (3, 1, F_DEV, D)).reshape(3 * F_DEV, D)
        window_value = lax.dynamic_slice(value_tiles, (time_block, region, zero_index, zero_index), (3, 1, F_DEV, D)).reshape(3 * F_DEV, D)
        query_frame = time_block * TT + jnp.arange(F_DEV, dtype=jnp.int32) // plane_cells
        key_frame = time_block * TT - TT + jnp.arange(3 * F_DEV, dtype=jnp.int32) // plane_cells
        distance = jnp.abs(query_frame[:, None] - key_frame[None, :])
        inside = (key_frame >= 0) & (key_frame < FRAMES)
        allowed = (distance[None, :, :] <= head_reach[:, None, None]) & inside[None, None, :]
        window_attention = attend_heads(query_rows, window_key, window_value, allowed)
        coarse_rows = lax.dynamic_index_in_dim(coarse_tiles, tile_index, 0, keepdims=False)
        spread = coarse_rows.reshape(TT, TH // 2, 1, TW // 2, 1, D)
        upsampled = jnp.broadcast_to(spread, (TT, TH // 2, 2, TW // 2, 2, D)).reshape(F_DEV, D)
        fine_rows = (window_attention + upsampled.astype(jnp.float32)).astype(jnp.bfloat16)
        cross_rows = attend_heads(query_rows, pooled_key, pooled_value, None).astype(jnp.bfloat16)
        return fine_rows, cross_rows

    fine_tiles, cross_tiles = lax.map(one_tile, jnp.arange(N_SEQ, dtype=jnp.int32))
    return fine_tiles.reshape(LF, D), cross_tiles.reshape(LF, D)
```

```python
import functools
import math

import jax
import jax.numpy as jnp
from jax import lax
from jax.experimental import pallas as pl
from jax.experimental.pallas import tpu as pltpu
from jax.sharding import PartitionSpec as P

HD = 128
TT = 4
TH = 4
TW = 8
NT = 8
HALO_F = 2
masked_score = -1e30
NT_DIMS = (((1,), (1,)), ((), ()))
NN_DIMS = (((1,), (0,)), ((), ()))


def remote(source, target, send_sem, recv_sem, device):
    return pltpu.make_async_remote_copy(
        src_ref=source,
        dst_ref=target,
        send_sem=send_sem,
        recv_sem=recv_sem,
        device_id={"seq": device},
        device_id_type=pl.DeviceIdType.MESH,
    )


def product(left, right, dims):
    return lax.dot_general(left, right, dims, preferred_element_type=jnp.float32)


def softmax_rows(scores):
    largest = jnp.max(scores, axis=-1, keepdims=True)
    exponent = jnp.exp(scores - largest)
    return exponent * (1.0 / jnp.sum(exponent, axis=-1, keepdims=True))


def kernel(
    n, groups, reach, cq, ck, cv, fq, fk, fv, out, cross,
    qbuf, kbuf, vbuf, abuf, rbuf, pbuf, before_k, before_v, after_k, after_v,
    q_send, kv_send, pass_send, pool_send, halo_send, back_send,
    q_recv, k_recv, v_recv, pool_recv, halo_recv, back_recv, local_sem,
):
    me = lax.axis_index("seq")
    blocks = n // groups
    pairs = n // 2
    core, pair = me % 2, me // 2
    sibling = 2 * pair + 1 - core
    mine, block = me // blocks, me % blocks
    width = cq.shape[1] // groups
    heads = width // HD
    fine_rows = fq.shape[0]
    coarse_rows = cq.shape[0]
    plane = TH * TW
    halo = HALO_F * plane
    across = n // NT
    tile = me // across
    scale = HD ** (-0.5)
    cells = TH // 2 * (TW // 2)

    def columns(group):
        return pl.ds(pl.multiple_of(group * width, HD), width)

    def peer(step):
        return 2 * ((pair + step) % pairs) + core

    def source(step):
        return 2 * ((pair + pairs - step) % pairs) + core

    def group_peer(step):
        return (mine + step) % groups

    barrier = pltpu.get_barrier_semaphore()

    @pl.loop(1, pairs)
    def _(step):
        pl.semaphore_signal(barrier, inc=1, device_id={"seq": peer(step)}, device_id_type=pl.DeviceIdType.MESH)

    pl.semaphore_signal(barrier, inc=1, device_id={"seq": sibling}, device_id_type=pl.DeviceIdType.MESH)
    pl.semaphore_wait(barrier, pairs)

    def key_copy(step):
        device = peer(step)
        return remote(ck.at[:, columns(device // blocks)], kbuf.at[me], kv_send.at[0, step], k_recv.at[me], device)

    def value_copy(step):
        device = peer(step)
        return remote(cv.at[:, columns(device // blocks)], vbuf.at[me], kv_send.at[1, step], v_recv.at[me], device)

    def query_copy(step):
        group = group_peer(step)
        return remote(cq.at[:, columns(group)], qbuf.at[mine], q_send.at[step], q_recv.at[mine], group * blocks + block)

    def pool_copy(step):
        return remote(pbuf.at[me], pbuf.at[me], pool_send.at[step], pool_recv.at[me], peer(step))

    def back_copy(step):
        group = group_peer(step)
        return remote(abuf.at[group], rbuf.at[mine], back_send.at[step], back_recv.at[mine], group * blocks + block)

    def pass_key(step):
        device = source(step)
        return remote(kbuf.at[device], kbuf.at[device], pass_send.at[0, step], k_recv.at[device], sibling)

    def pass_value(step):
        device = source(step)
        return remote(vbuf.at[device], vbuf.at[device], pass_send.at[1, step], v_recv.at[device], sibling)

    def pass_pool(step):
        device = source(step)
        return remote(pbuf.at[device], pbuf.at[device], pass_send.at[2, step], pool_recv.at[device], sibling)

    own_k = pltpu.make_async_copy(ck.at[:, columns(mine)], kbuf.at[me], local_sem.at[0])
    own_v = pltpu.make_async_copy(cv.at[:, columns(mine)], vbuf.at[me], local_sem.at[1])
    own_q = pltpu.make_async_copy(cq.at[:, columns(mine)], qbuf.at[mine], local_sem.at[2])
    own_k.start()
    own_v.start()
    own_q.start()

    @pl.loop(1, pairs)
    def _(step):
        key_copy(step).start()
        value_copy(step).start()

    @pl.loop(1, groups)
    def _(step):
        query_copy(step).start()

    pool_rows = 4 * TT
    row = lax.broadcasted_iota(jnp.int32, (pool_rows, coarse_rows), 0)
    col = lax.broadcasted_iota(jnp.int32, (pool_rows, coarse_rows), 1)
    member = jnp.where(row % TT == col // cells, 1.0, 0.0).astype(jnp.bfloat16)

    @pl.loop(0, groups)
    def _(group):
        cols = columns(group)
        pooled_k = product(member, ck[:, cols], NN_DIMS) * cells ** (-0.5)
        pooled_v = product(member, cv[:, cols], NN_DIMS) * cells ** (-0.5)
        which = lax.broadcasted_iota(jnp.int32, pooled_k.shape, 0) // TT
        pooled = jnp.where(which < 2, pooled_k, pooled_v)
        high = pooled.astype(jnp.bfloat16).astype(jnp.float32)
        pbuf[me, :, cols] = jnp.where(which % 2 == 0, high, pooled - high).astype(jnp.bfloat16)

    own_k.wait()
    own_v.wait()
    own_q.wait()
    pass_key(0).start()
    pass_value(0).start()

    @pl.loop(1, pairs)
    def _(step):
        pool_copy(step).start()

    pass_pool(0).start()

    def halo_copies(group, which):
        cols = columns(group)
        if which == 0:
            rows, device, targets = pl.ds(fine_rows - halo, halo), me + across, (before_k, before_v)
        else:
            rows, device, targets = pl.ds(0, halo), me - across, (after_k, after_v)
        return [
            remote(
                fine.at[rows, cols], target.at[:, cols],
                halo_send.at[2 * which + index, group], halo_recv.at[2 * which + index, group], device,
            )
            for index, (fine, target) in enumerate(zip((fk, fv), targets))
        ]

    @pl.loop(0, groups)
    def _(group):
        @pl.when(tile < NT - 1)
        def _():
            for copy in halo_copies(group, 0):
                copy.start()

        @pl.when(tile > 0)
        def _():
            for copy in halo_copies(group, 1):
                copy.start()

    @pl.when(tile == 0)
    def _():
        before_k[...] = jnp.zeros_like(before_k)
        before_v[...] = jnp.zeros_like(before_v)

    @pl.when(tile == NT - 1)
    def _():
        after_k[...] = jnp.zeros_like(after_k)
        after_v[...] = jnp.zeros_like(after_v)

    @pl.loop(1, pairs)
    def _(step):
        device = source(step)
        remote(kbuf.at[device], kbuf.at[device], kv_send.at[0, step], k_recv.at[device], device).wait_recv()
        pass_key(step).start()
        remote(vbuf.at[device], vbuf.at[device], kv_send.at[1, step], v_recv.at[device], device).wait_recv()
        pass_value(step).start()

    @pl.loop(1, groups)
    def _(step):
        group = group_peer(step)
        remote(qbuf.at[group], qbuf.at[group], q_send.at[step], q_recv.at[group], group * blocks + block).wait_recv()

    def other(step):
        return 2 * ((pair + pairs - step) % pairs) + 1 - core

    @pl.loop(0, pairs)
    def _(step):
        device = other(step)
        remote(kbuf.at[device], kbuf.at[device], pass_send.at[0, step], k_recv.at[device], sibling).wait_recv()
        remote(vbuf.at[device], vbuf.at[device], pass_send.at[1, step], v_recv.at[device], sibling).wait_recv()

    for head in range(heads):
        lanes = slice(head * HD, (head + 1) * HD)
        queries = qbuf[:, :, lanes].reshape(groups * coarse_rows, HD)
        keys = kbuf[:, :, lanes].reshape(n * coarse_rows, HD)
        values = vbuf[:, :, lanes].reshape(n * coarse_rows, HD)
        weights = softmax_rows(product(queries, keys, NT_DIMS) * scale).astype(jnp.bfloat16)
        mixed = product(weights, values, NN_DIMS).astype(jnp.bfloat16)
        abuf[:, :, lanes] = mixed.reshape(groups, coarse_rows, HD)

    @pl.loop(1, groups)
    def _(step):
        back_copy(step).start()

    rbuf[mine] = abuf[mine]

    @pl.loop(1, pairs)
    def _(step):
        device = source(step)
        remote(pbuf.at[device], pbuf.at[device], pool_send.at[step], pool_recv.at[device], device).wait_recv()
        pass_pool(step).start()

    @pl.loop(0, pairs)
    def _(step):
        device = other(step)
        remote(pbuf.at[device], pbuf.at[device], pass_send.at[2, step], pool_recv.at[device], sibling).wait_recv()

    pooled_total = n * pool_rows
    place = lax.broadcasted_iota(jnp.int32, (fine_rows, pooled_total), 1) % pool_rows

    @pl.loop(0, groups)
    def _(group):
        for head in range(heads):
            cols = pl.ds(pl.multiple_of(group * width + head * HD, HD), HD)
            pooled = pbuf[:, :, cols].reshape(pooled_total, HD)
            scores = product(fq[:, cols], pooled, NT_DIMS)
            scores = (scores + pltpu.roll(scores, pooled_total - TT, 1)) * scale
            weights = softmax_rows(jnp.where(place < TT, scores, masked_score))
            weights = weights.astype(jnp.bfloat16).astype(jnp.float32)
            spread = pltpu.roll(weights, 2 * TT, 1) + pltpu.roll(weights, 3 * TT, 1)
            cross[:, cols] = product(spread.astype(jnp.bfloat16), pooled, NN_DIMS).astype(jnp.bfloat16)

    window = fine_rows + 2 * halo
    query_frame = lax.broadcasted_iota(jnp.int32, (fine_rows, window), 0) // plane
    key_frame = lax.broadcasted_iota(jnp.int32, (fine_rows, window), 1) // plane - HALO_F
    distance = jnp.abs(query_frame - key_frame)
    absolute = key_frame + tile * TT
    distance = jnp.where((absolute >= 0) & (absolute < NT * TT), distance, NT * TT)
    fine_row = lax.broadcasted_iota(jnp.int32, (fine_rows, coarse_rows), 0)
    coarse_row = lax.broadcasted_iota(jnp.int32, (fine_rows, coarse_rows), 1)
    parent = (fine_row // plane * (TH // 2) + fine_row % plane // TW // 2) * (TW // 2) + fine_row % TW // 2
    lift = jnp.where(parent == coarse_row, 1.0, 0.0).astype(jnp.bfloat16)

    @pl.loop(0, groups)
    def _(group):
        @pl.when(group != mine)
        def _():
            remote(
                rbuf.at[group], rbuf.at[group], back_send.at[0], back_recv.at[group], group * blocks + block
            ).wait_recv()

        @pl.when(tile > 0)
        def _():
            for copy in halo_copies(group, 0):
                copy.wait_recv()

        @pl.when(tile < NT - 1)
        def _():
            for copy in halo_copies(group, 1):
                copy.wait_recv()

        raised = product(lift, rbuf[group], NN_DIMS)
        for head in range(heads):
            cols = pl.ds(pl.multiple_of(group * width + head * HD, HD), HD)
            keys = jnp.concatenate([before_k[:, cols], fk[:, cols], after_k[:, cols]], axis=0)
            values = jnp.concatenate([before_v[:, cols], fv[:, cols], after_v[:, cols]], axis=0)
            scores = product(fq[:, cols], keys, NT_DIMS) * scale
            scores = jnp.where(distance <= reach[group * heads + head], scores, masked_score)
            weights = softmax_rows(scores).astype(jnp.bfloat16)
            mixed = product(weights, values, NN_DIMS)
            out[:, cols] = (mixed + raised[:, head * HD : (head + 1) * HD]).astype(jnp.bfloat16)

    @pl.loop(1, pairs)
    def _(step):
        key_copy(step).wait_send()
        value_copy(step).wait_send()
        pool_copy(step).wait_send()

    @pl.loop(0, pairs)
    def _(step):
        pass_key(step).wait_send()
        pass_value(step).wait_send()
        pass_pool(step).wait_send()

    @pl.loop(1, groups)
    def _(step):
        query_copy(step).wait_send()
        back_copy(step).wait_send()

    @pl.loop(0, groups)
    def _(group):
        @pl.when(tile < NT - 1)
        def _():
            for copy in halo_copies(group, 0):
                copy.wait_send()

        @pl.when(tile > 0)
        def _():
            for copy in halo_copies(group, 1):
                copy.wait_send()


def shards(coarse_query, coarse_key, coarse_value, fine_query, fine_key, fine_value, head_reach):
    n = lax.axis_size("seq")
    coarse_rows, model_width = coarse_query.shape
    fine_rows = fine_query.shape[0]
    head_count = model_width // HD
    groups = math.gcd(head_count, n)
    width = model_width // groups
    pairs = n // 2
    halo = HALO_F * TH * TW
    bf16 = jnp.bfloat16
    dma = pltpu.SemaphoreType.DMA
    vmem = pl.BlockSpec(memory_space=pltpu.VMEM)
    window = fine_rows + 2 * halo
    work = 4 * model_width * (fine_rows * (window + 16 * n) + groups * coarse_rows * n * coarse_rows // groups)
    return pl.pallas_call(
        functools.partial(kernel, n, groups),
        out_shape=[jax.ShapeDtypeStruct((fine_rows, model_width), bf16)] * 2,
        in_specs=[pl.BlockSpec(memory_space=pltpu.SMEM)] + [vmem] * 6,
        out_specs=[vmem] * 2,
        scratch_shapes=[
            pltpu.VMEM((groups, coarse_rows, width), bf16),
            pltpu.VMEM((n, coarse_rows, width), bf16),
            pltpu.VMEM((n, coarse_rows, width), bf16),
            pltpu.VMEM((groups, coarse_rows, width), bf16),
            pltpu.VMEM((groups, coarse_rows, width), bf16),
            pltpu.VMEM((n, 4 * TT, model_width), bf16),
            pltpu.VMEM((halo, model_width), bf16),
            pltpu.VMEM((halo, model_width), bf16),
            pltpu.VMEM((halo, model_width), bf16),
            pltpu.VMEM((halo, model_width), bf16),
            dma((groups,)), dma((2, pairs)), dma((3, pairs)), dma((pairs,)), dma((4, groups)), dma((groups,)),
            dma((groups,)), dma((n,)), dma((n,)), dma((n,)), dma((4, groups)), dma((groups,)), dma((3,)),
        ],
        compiler_params=pltpu.CompilerParams(
            collective_id=0, has_side_effects=True, vmem_limit_bytes=52 * 1024 * 1024
        ),
        cost_estimate=pl.CostEstimate(flops=work, bytes_accessed=12 * fine_rows * model_width, transcendentals=0),
    )(head_reach, coarse_query, coarse_key, coarse_value, fine_query, fine_key, fine_value)


def solution(mesh):
    rows = P(("group", "seq"), None)
    return jax.shard_map(
        shards, mesh=mesh, in_specs=(rows,) * 6 + (P(),), out_specs=(rows, rows), check_vma=False
    )
```

```python
import functools
import math

import jax
import jax.numpy as jnp
from jax import lax
from jax.experimental import pallas as pl
from jax.experimental.pallas import tpu as pltpu
from jax.sharding import PartitionSpec as P

HD = 128
TT = 4
TH = 4
TW = 8
NT = 8
HALO_F = 2
masked_score = -1e30
NT_DIMS = (((1,), (1,)), ((), ()))
NN_DIMS = (((1,), (0,)), ((), ()))
TN_DIMS = (((0,), (0,)), ((), ()))


def remote(source, target, send_sem, recv_sem, device):
    return pltpu.make_async_remote_copy(
        src_ref=source,
        dst_ref=target,
        send_sem=send_sem,
        recv_sem=recv_sem,
        device_id={"seq": device},
        device_id_type=pl.DeviceIdType.MESH,
    )


def inner_size(pairs):
    return 1


def product(left, right, dims):
    return lax.dot_general(left, right, dims, preferred_element_type=jnp.float32)


def softmax_rows(scores):
    largest = jnp.max(scores, axis=-1, keepdims=True)
    exponent = jnp.exp(scores - largest)
    return exponent * (1.0 / jnp.sum(exponent, axis=-1, keepdims=True))


def kernel(
    n, groups, reach, cq, ck_far, cv_far, fq_far, fk_far, fv_far, out, cross,
    ck, cv, fq, fk, fv,
    qbuf, kbuf, vbuf, abuf, rbuf, pbuf, before_k, before_v, after_k, after_v,
    q_send, kv_send, pass_send, pool_send, across_send, halo_send, back_send,
    q_recv, k_recv, v_recv, pool_recv, halo_recv, back_recv, local_sem,
):
    me = lax.axis_index("seq")
    blocks = n // groups
    pairs = n // 2
    inner = inner_size(pairs)
    outer = pairs // inner
    core, pair = me % 2, me // 2
    far, near = pair // inner, pair % inner
    sibling = 2 * pair + 1 - core
    mine, block = me // blocks, me % blocks
    width = cq.shape[1] // groups
    heads = width // HD
    fine_rows = fq.shape[0]
    coarse_rows = cq.shape[0]
    plane = TH * TW
    halo = HALO_F * plane
    across = n // NT
    tile = me // across
    scale = HD ** (-0.5)
    cells = TH // 2 * (TW // 2)

    def columns(group):
        return pl.ds(pl.multiple_of(group * width, HD), width)

    def peer(step):
        return 2 * ((pair + step) % pairs) + core

    def source(step):
        return 2 * ((pair + pairs - step) % pairs) + core

    def group_peer(step):
        return (mine + step) % groups

    staged = [
        pltpu.make_async_copy(far_ref, near_ref, local_sem.at[3 + index])
        for index, (far_ref, near_ref) in enumerate(
            zip((ck_far, cv_far, fq_far, fk_far, fv_far), (ck, cv, fq, fk, fv))
        )
    ]
    barrier = pltpu.get_barrier_semaphore()

    @pl.loop(1, pairs)
    def _(step):
        pl.semaphore_signal(barrier, inc=1, device_id={"seq": peer(step)}, device_id_type=pl.DeviceIdType.MESH)

    pl.semaphore_signal(barrier, inc=1, device_id={"seq": sibling}, device_id_type=pl.DeviceIdType.MESH)
    own_k = pltpu.make_async_copy(ck_far.at[:, columns(mine)], kbuf.at[me], local_sem.at[0])
    own_v = pltpu.make_async_copy(cv_far.at[:, columns(mine)], vbuf.at[me], local_sem.at[1])
    own_q = pltpu.make_async_copy(cq.at[:, columns(mine)], qbuf.at[mine], local_sem.at[2])
    own_k.start()
    own_v.start()
    own_q.start()
    for copy in staged:
        copy.start()
    pl.semaphore_wait(barrier, pairs)

    def key_copy(step):
        device = peer(step)
        return remote(ck_far.at[:, columns(device // blocks)], kbuf.at[me], kv_send.at[0, step], k_recv.at[me], device)

    def value_copy(step):
        device = peer(step)
        return remote(cv_far.at[:, columns(device // blocks)], vbuf.at[me], kv_send.at[1, step], v_recv.at[me], device)

    def query_copy(step):
        group = group_peer(step)
        return remote(cq.at[:, columns(group)], qbuf.at[mine], q_send.at[step], q_recv.at[mine], group * blocks + block)

    def pool_copy(step):
        device = 2 * ((far + step) % outer * inner + near) + core
        return remote(pbuf.at[me], pbuf.at[me], pool_send.at[step], pool_recv.at[me], device)

    def pool_origin(step, shift):
        return 2 * ((far + outer - step) % outer * inner + (near + inner - shift) % inner) + core

    def pool_across(step, shift):
        held = pool_origin(step, 0)
        device = 2 * (far * inner + (near + shift) % inner) + core
        return remote(pbuf.at[held], pbuf.at[held], across_send.at[step, shift], pool_recv.at[held], device)

    def pool_arrived(step, shift):
        held = pool_origin(step, shift)
        return remote(pbuf.at[held], pbuf.at[held], pool_send.at[0], pool_recv.at[held], held)

    def back_copy(step):
        group = group_peer(step)
        return remote(abuf.at[group], rbuf.at[mine], back_send.at[step], back_recv.at[mine], group * blocks + block)

    def pass_key(step):
        device = source(step)
        return remote(kbuf.at[device], kbuf.at[device], pass_send.at[0, step], k_recv.at[device], sibling)

    def pass_value(step):
        device = source(step)
        return remote(vbuf.at[device], vbuf.at[device], pass_send.at[1, step], v_recv.at[device], sibling)

    def pass_pool(step, shift):
        device = pool_origin(step, shift)
        return remote(pbuf.at[device], pbuf.at[device], pass_send.at[2, step * inner + shift], pool_recv.at[device], sibling)

    @pl.loop(1, pairs)
    def _(step):
        key_copy(step).start()
        value_copy(step).start()

    @pl.loop(1, groups)
    def _(step):
        query_copy(step).start()

    staged[0].wait()
    staged[1].wait()

    pool_rows = 4 * TT
    row = lax.broadcasted_iota(jnp.int32, (pool_rows, coarse_rows), 0)
    col = lax.broadcasted_iota(jnp.int32, (pool_rows, coarse_rows), 1)
    member = jnp.where(row % TT == col // cells, 1.0, 0.0).astype(jnp.bfloat16)

    @pl.loop(0, groups)
    def _(group):
        cols = columns(group)
        pooled_k = product(member, ck[:, cols], NN_DIMS) * cells ** (-0.5)
        pooled_v = product(member, cv[:, cols], NN_DIMS) * cells ** (-0.5)
        which = lax.broadcasted_iota(jnp.int32, pooled_k.shape, 0) // TT
        pooled = jnp.where(which < 2, pooled_k, pooled_v)
        high = pooled.astype(jnp.bfloat16).astype(jnp.float32)
        pbuf[me, :, cols] = jnp.where(which % 2 == 0, high, pooled - high).astype(jnp.bfloat16)

    own_k.wait()
    own_v.wait()
    own_q.wait()
    pass_key(0).start()
    pass_value(0).start()

    @pl.loop(1, outer)
    def _(step):
        pool_copy(step).start()

    @pl.loop(1, inner)
    def _(shift):
        pool_across(0, shift).start()

    pass_pool(0, 0).start()

    for copy in staged[3:]:
        copy.wait()

    def halo_copies(group, which):
        cols = columns(group)
        if which == 0:
            rows, device, targets = pl.ds(fine_rows - halo, halo), me + across, (before_k, before_v)
        else:
            rows, device, targets = pl.ds(0, halo), me - across, (after_k, after_v)
        return [
            remote(
                fine.at[rows, cols], target.at[:, cols],
                halo_send.at[2 * which + index, group], halo_recv.at[2 * which + index, group], device,
            )
            for index, (fine, target) in enumerate(zip((fk, fv), targets))
        ]

    @pl.loop(0, 3 * groups // 4)
    def _(group):
        @pl.when(tile < NT - 1)
        def _():
            for copy in halo_copies(group, 0):
                copy.start()

        @pl.when(tile > 0)
        def _():
            for copy in halo_copies(group, 1):
                copy.start()

    @pl.when(tile == 0)
    def _():
        before_k[...] = jnp.zeros_like(before_k)
        before_v[...] = jnp.zeros_like(before_v)

    @pl.when(tile == NT - 1)
    def _():
        after_k[...] = jnp.zeros_like(after_k)
        after_v[...] = jnp.zeros_like(after_v)

    @pl.loop(1, pairs)
    def _(step):
        device = source(step)
        remote(kbuf.at[device], kbuf.at[device], kv_send.at[0, step], k_recv.at[device], device).wait_recv()
        pass_key(step).start()
        remote(vbuf.at[device], vbuf.at[device], kv_send.at[1, step], v_recv.at[device], device).wait_recv()
        pass_value(step).start()

    @pl.loop(1, groups)
    def _(step):
        group = group_peer(step)
        remote(qbuf.at[group], qbuf.at[group], q_send.at[step], q_recv.at[group], group * blocks + block).wait_recv()

    def other(step):
        return 2 * ((pair + pairs - step) % pairs) + 1 - core

    @pl.loop(0, pairs)
    def _(step):
        device = other(step)
        remote(kbuf.at[device], kbuf.at[device], pass_send.at[0, step], k_recv.at[device], sibling).wait_recv()
        remote(vbuf.at[device], vbuf.at[device], pass_send.at[1, step], v_recv.at[device], sibling).wait_recv()

    @pl.loop(1, outer)
    def _(step):
        pool_arrived(step, 0).wait_recv()

        @pl.loop(1, inner)
        def _(shift):
            pool_across(step, shift).start()

        pass_pool(step, 0).start()

    for head in range(heads):
        lanes = slice(head * HD, (head + 1) * HD)
        queries = qbuf[:, :, lanes].reshape(groups * coarse_rows, HD)
        keys = kbuf[:, :, lanes].reshape(n * coarse_rows, HD)
        values = vbuf[:, :, lanes].reshape(n * coarse_rows, HD)
        weights = softmax_rows(product(queries, keys, NT_DIMS) * scale).astype(jnp.bfloat16)
        mixed = product(weights, values, NN_DIMS).astype(jnp.bfloat16)
        abuf[:, :, lanes] = mixed.reshape(groups, coarse_rows, HD)

    @pl.loop(1, groups)
    def _(step):
        back_copy(step).start()

    @pl.loop(3 * groups // 4, groups)
    def _(group):
        @pl.when(tile < NT - 1)
        def _():
            for copy in halo_copies(group, 0):
                copy.start()

        @pl.when(tile > 0)
        def _():
            for copy in halo_copies(group, 1):
                copy.start()

    rbuf[mine] = abuf[mine]

    @pl.loop(0, outer)
    def _(step):
        @pl.loop(1, inner)
        def _(shift):
            pool_arrived(step, shift).wait_recv()
            pass_pool(step, shift).start()

    @pl.loop(0, pairs)
    def _(step):
        device = other(step)
        remote(pbuf.at[device], pbuf.at[device], pass_send.at[2, step], pool_recv.at[device], sibling).wait_recv()

    staged[2].wait()
    pooled_total = n * pool_rows

    @pl.loop(0, groups)
    def _(group):
        for head in range(heads):
            cols = pl.ds(pl.multiple_of(group * width + head * HD, HD), HD)
            pooled = pbuf[:, :, cols].reshape(pooled_total, HD)
            scores = product(pooled, fq[:, cols], NT_DIMS).reshape(n, pool_rows, fine_rows)[:, : 2 * TT]
            scores = (scores + pltpu.roll(scores, TT, 1)) * scale
            largest = jnp.max(scores, axis=(0, 1), keepdims=True)
            exponent = jnp.exp(scores - largest)
            weights = exponent * (2.0 / jnp.sum(exponent, axis=(0, 1), keepdims=True))
            spread = jnp.concatenate([jnp.zeros_like(weights), weights], axis=1)
            spread = spread.reshape(pooled_total, fine_rows).astype(jnp.bfloat16)
            cross[:, cols] = product(spread, pooled, TN_DIMS).astype(jnp.bfloat16)

    window = fine_rows + 2 * halo
    query_frame = lax.broadcasted_iota(jnp.int32, (fine_rows, window), 0) // plane
    key_frame = lax.broadcasted_iota(jnp.int32, (fine_rows, window), 1) // plane - HALO_F
    distance = jnp.abs(query_frame - key_frame)
    absolute = key_frame + tile * TT
    distance = jnp.where((absolute >= 0) & (absolute < NT * TT), distance, NT * TT)
    fine_row = lax.broadcasted_iota(jnp.int32, (fine_rows, coarse_rows), 0)
    coarse_row = lax.broadcasted_iota(jnp.int32, (fine_rows, coarse_rows), 1)
    parent = (fine_row // plane * (TH // 2) + fine_row % plane // TW // 2) * (TW // 2) + fine_row % TW // 2
    lift = jnp.where(parent == coarse_row, 1.0, 0.0).astype(jnp.bfloat16)

    @pl.loop(0, groups)
    def _(group):
        @pl.when(group != mine)
        def _():
            remote(
                rbuf.at[group], rbuf.at[group], back_send.at[0], back_recv.at[group], group * blocks + block
            ).wait_recv()

        @pl.when(tile > 0)
        def _():
            for copy in halo_copies(group, 0):
                copy.wait_recv()

        @pl.when(tile < NT - 1)
        def _():
            for copy in halo_copies(group, 1):
                copy.wait_recv()

        raised = product(lift, rbuf[group], NN_DIMS)
        for head in range(heads):
            cols = pl.ds(pl.multiple_of(group * width + head * HD, HD), HD)
            keys = jnp.concatenate([before_k[:, cols], fk[:, cols], after_k[:, cols]], axis=0)
            values = jnp.concatenate([before_v[:, cols], fv[:, cols], after_v[:, cols]], axis=0)
            scores = product(fq[:, cols], keys, NT_DIMS) * scale
            scores = jnp.where(distance <= reach[group * heads + head], scores, masked_score)
            weights = softmax_rows(scores).astype(jnp.bfloat16)
            mixed = product(weights, values, NN_DIMS)
            out[:, cols] = (mixed + raised[:, head * HD : (head + 1) * HD]).astype(jnp.bfloat16)

    @pl.loop(1, pairs)
    def _(step):
        key_copy(step).wait_send()
        value_copy(step).wait_send()

    @pl.loop(0, pairs)
    def _(step):
        pass_key(step).wait_send()
        pass_value(step).wait_send()
        pass_pool(step // inner, step % inner).wait_send()

    @pl.loop(0, outer)
    def _(step):
        @pl.when(step > 0)
        def _():
            pool_copy(step).wait_send()

        @pl.loop(1, inner)
        def _(shift):
            pool_across(step, shift).wait_send()

    @pl.loop(1, groups)
    def _(step):
        query_copy(step).wait_send()
        back_copy(step).wait_send()

    @pl.loop(0, groups)
    def _(group):
        @pl.when(tile < NT - 1)
        def _():
            for copy in halo_copies(group, 0):
                copy.wait_send()

        @pl.when(tile > 0)
        def _():
            for copy in halo_copies(group, 1):
                copy.wait_send()


def shards(coarse_query, coarse_key, coarse_value, fine_query, fine_key, fine_value, head_reach):
    n = lax.axis_size("seq")
    coarse_rows, model_width = coarse_query.shape
    fine_rows = fine_query.shape[0]
    head_count = model_width // HD
    groups = math.gcd(head_count, n)
    width = model_width // groups
    pairs = n // 2
    inner = inner_size(pairs)
    outer = pairs // inner
    halo = HALO_F * TH * TW
    bf16 = jnp.bfloat16
    dma = pltpu.SemaphoreType.DMA
    vmem = pl.BlockSpec(memory_space=pltpu.VMEM)
    window = fine_rows + 2 * halo
    work = 4 * model_width * (fine_rows * (window + 16 * n) + groups * coarse_rows * n * coarse_rows // groups)
    return pl.pallas_call(
        functools.partial(kernel, n, groups),
        out_shape=[jax.ShapeDtypeStruct((fine_rows, model_width), bf16)] * 2,
        in_specs=[pl.BlockSpec(memory_space=pltpu.SMEM)] + [pl.BlockSpec(memory_space=pl.ANY)] * 6,
        out_specs=[vmem] * 2,
        scratch_shapes=[
            pltpu.VMEM((coarse_rows, model_width), bf16),
            pltpu.VMEM((coarse_rows, model_width), bf16),
            pltpu.VMEM((fine_rows, model_width), bf16),
            pltpu.VMEM((fine_rows, model_width), bf16),
            pltpu.VMEM((fine_rows, model_width), bf16),
            pltpu.VMEM((groups, coarse_rows, width), bf16),
            pltpu.VMEM((n, coarse_rows, width), bf16),
            pltpu.VMEM((n, coarse_rows, width), bf16),
            pltpu.VMEM((groups, coarse_rows, width), bf16),
            pltpu.VMEM((groups, coarse_rows, width), bf16),
            pltpu.VMEM((n, 4 * TT, model_width), bf16),
            pltpu.VMEM((halo, model_width), bf16),
            pltpu.VMEM((halo, model_width), bf16),
            pltpu.VMEM((halo, model_width), bf16),
            pltpu.VMEM((halo, model_width), bf16),
            dma((groups,)), dma((2, pairs)), dma((3, pairs)), dma((outer,)), dma((outer, inner)),
            dma((4, groups)), dma((groups,)),
            dma((groups,)), dma((n,)), dma((n,)), dma((n,)), dma((4, groups)), dma((groups,)), dma((8,)),
        ],
        compiler_params=pltpu.CompilerParams(
            collective_id=0, has_side_effects=True, vmem_limit_bytes=52 * 1024 * 1024
        ),
        cost_estimate=pl.CostEstimate(flops=work, bytes_accessed=12 * fine_rows * model_width, transcendentals=0),
    )(head_reach, coarse_query, coarse_key, coarse_value, fine_query, fine_key, fine_value)


def solution(mesh):
    rows = P(("group", "seq"), None)
    return jax.shard_map(
        shards, mesh=mesh, in_specs=(rows,) * 6 + (P(),), out_specs=(rows, rows), check_vma=False
    )
```
